256 devices in a mesh: ctx: 32 (over x, z), head: 8 (over y, core).
Axes of the slice: x: 4, y: 4, z: 8, core: 2. Of those that a mesh axis runs over, the one named last changes fastest.
Arguments:
- queries: bfloat16 [16384, 4096], P('ctx', 'head'), may hold values from -5 to 5
- key_rows: bfloat16 [16384, 1024], P('ctx', 'head'), may hold values from -5 to 5
- value_rows: bfloat16 [16384, 1024], P('ctx', 'head'), may hold values from -6 to 6
- slash_offsets: int32 [32, 4], P('head'), may hold values from 0 to 8, as said below
- union_blocks: int32 [8, 32, 2], P('head'), may hold values from 0 to 7, as said below
- head_picks: int32 [32, 32, 1], P('head'), may hold values from 0 to 1, as said below
- owner_counts: int32 [32, 32], P('head'), may hold values from 0 to 1, as said below
- out_weight: bfloat16 [4096, 4096], P(None, 'head'), may hold values from -0.09375 to 0.09375
Outputs:
- projected: bfloat16 [16384, 4096], P('ctx', 'head')
The draws below stay inside these ranges and needn't reach their ends.
Inputs may be any that keep to these rules, and one draw needn't show every extreme that they name: `slash_offsets`: each head's offsets are distinct and include 0 and 8. `union_blocks`: the 2 entries of each KV head and sequence block are distinct. `head_picks`: the 1 entries of each query head and sequence block are distinct. `owner_counts`: equal to 1 for sequence block 0.
All inputs are finite; a program needn't handle non-finite values.
Results may differ from the reference program's by a relative error of at most 0.0056.
Values may be sent and summed in bfloat16 or wider, within the bound.
A program may use at most 128 MiB of HBM per device.

```python
import jax
import jax.numpy as jnp
from jax import lax

D = 4096
HQ = 32
KVH = 8
HEAD_SIZE = 128
BLOCK_TOKENS = 64
NS = 4
VPER = 1
UNION = 2
TOK_DEV = 512
SEQ = 16384


def paired_draw(key):
    base_key = jax.random.fold_in(key, 7)
    keys_list = jax.random.split(base_key, 2)
    query_draw = jax.random.truncated_normal(keys_list[0], -4.5, 4.5, (SEQ, HQ * HEAD_SIZE), jnp.float32)
    key_draw = jax.random.truncated_normal(keys_list[1], -4.5, 4.5, (SEQ, KVH * HEAD_SIZE), jnp.float32)
    return (query_draw, key_draw)


def draw_queries(key, part):
    return paired_draw(key)[0].astype(jnp.bfloat16)


def draw_key_rows(key, part):
    return paired_draw(key)[1].astype(jnp.bfloat16)


def distinct_order(key, shape):
    width = shape[-1]
    scores = jax.random.randint(key, shape, 0, 65536) * width + jnp.arange(width, dtype=jnp.int32)
    return jnp.argsort(scores, axis=-1, stable=True).astype(jnp.int32)


def draw_slash_offsets(key, part):
    reach = TOK_DEV // BLOCK_TOKENS
    orders = distinct_order(jax.random.fold_in(key, 3), (HQ, reach - 1))
    middle = orders[:, :NS - 2] + 1
    first = jnp.zeros((HQ, 1), jnp.int32)
    farthest = jnp.full((HQ, 1), reach, jnp.int32)
    return jnp.concatenate([first, farthest, middle], axis=1).astype(jnp.int32)


def draw_union_blocks(key, part):
    orders = distinct_order(jax.random.fold_in(key, 5), (KVH, SEQ // TOK_DEV, TOK_DEV // BLOCK_TOKENS))
    return orders[:, :, :UNION]


def draw_head_picks(key, part):
    orders = distinct_order(jax.random.fold_in(key, 9), (HQ, SEQ // TOK_DEV, UNION))
    return orders[:, :, :VPER]


def draw_owner_counts(key, part):
    counts = jax.random.randint(jax.random.fold_in(key, 13), (HQ, SEQ // TOK_DEV), 0, VPER + 1)
    return counts.at[:, 0].set(VPER).astype(jnp.int32)


def block_scale(own_key, dims, pieces, least, largest):
    factor_of, own = 1.0, jax.random.fold_in(own_key, 6)
    for axis_at, shards_of in pieces:
        draws = jnp.exp(jax.random.uniform(jax.random.fold_in(own, axis_at), (shards_of,), jnp.float32, least / len(pieces), largest / len(pieces)))
        factor_of = factor_of * jnp.repeat(draws, dims[axis_at] // shards_of).reshape([-1 if axis == axis_at else 1 for axis in range(len(dims))])
    return factor_of


def bell_draw(rng, dims, spread, most, shards=(), kind=jnp.bfloat16):
    result = spread * jax.random.normal(rng, dims, jnp.float32)
    if shards:
        result = result * block_scale(rng, dims, shards, -0.22, 0.18)
    return jnp.clip(result, -most, most).astype(kind)


def setup_inputs(seed: int = 0) -> dict:
    key_list = jax.random.split(jax.random.key(seed), 9)
    return {
        "queries": draw_queries(jax.random.fold_in(key_list[8], 71), 0),
        "key_rows": draw_key_rows(jax.random.fold_in(key_list[8], 71), 0),
        "value_rows": bell_draw(key_list[2], (SEQ, KVH * HEAD_SIZE), 1.0, 6.0, ((0, 32), (1, 8))),
        "slash_offsets": draw_slash_offsets(jax.random.fold_in(key_list[8], 71), 0),
        "union_blocks": draw_union_blocks(jax.random.fold_in(key_list[8], 71), 0),
        "head_picks": draw_head_picks(jax.random.fold_in(key_list[8], 71), 0),
        "owner_counts": draw_owner_counts(jax.random.fold_in(key_list[8], 71), 0),
        "out_weight": bell_draw(key_list[7], (HQ * HEAD_SIZE, D), (HQ * HEAD_SIZE) ** -0.5, 0.09375, ((1, 8),)),
    }


def attend(vert_scores, vert_mask, diagonal_scores, slash_mask, vert_values, diagonal_values, count_of_blocks):
    masked_vert = jnp.where(vert_mask, vert_scores, -1e30)
    masked_slash = jnp.where(slash_mask, diagonal_scores, -1e30)
    peak = jnp.maximum(jnp.max(masked_vert, axis=-1, keepdims=True), jnp.max(masked_slash, axis=-1, keepdims=True))
    weight_vert = jnp.exp(masked_vert - peak)
    weight_slash = jnp.exp(masked_slash - peak)
    total = jnp.sum(weight_vert, axis=-1, keepdims=True) + jnp.sum(weight_slash, axis=-1, keepdims=True)
    prob_vert = weight_vert.astype(jnp.bfloat16)
    slash_probability = lax.optimization_barrier(weight_slash.astype(jnp.bfloat16)).astype(jnp.float32)
    numer = jnp.dot(prob_vert, vert_values, preferred_element_type=jnp.float32)
    slash_probability = slash_probability.reshape(count_of_blocks, BLOCK_TOKENS, NS, BLOCK_TOKENS)
    diagonal_portion = jnp.einsum("wojf,wjfl->wol", slash_probability, diagonal_values.astype(jnp.float32), precision=lax.Precision.HIGHEST)
    numer = numer + diagonal_portion.reshape(count_of_blocks * BLOCK_TOKENS, HEAD_SIZE)
    return (numer / total).astype(jnp.bfloat16)


def reference(queries, key_rows, value_rows, slash_offsets, union_blocks, head_picks, owner_counts, out_weight):
    group_size = HQ // KVH
    per_dev = TOK_DEV // BLOCK_TOKENS
    count_of_blocks = SEQ // BLOCK_TOKENS
    scale_of_scores = jnp.float32(HEAD_SIZE ** -0.5)
    inner_offset = jnp.arange(BLOCK_TOKENS, dtype=jnp.int32)
    query_place = jnp.arange(SEQ, dtype=jnp.int32)
    query_block = jnp.arange(count_of_blocks, dtype=jnp.int32)
    owner_base = jnp.arange(SEQ // TOK_DEV, dtype=jnp.int32)[:, None] * per_dev
    query_all = queries.reshape(SEQ, HQ, HEAD_SIZE)
    key_all = key_rows.reshape(SEQ, KVH, HEAD_SIZE)
    value_all = value_rows.reshape(SEQ, KVH, HEAD_SIZE)

    def one_head(head_index):
        kv_index = (head_index // group_size).astype(jnp.int32)
        query_head = lax.dynamic_index_in_dim(query_all, head_index, 1, keepdims=False)
        key_head = lax.dynamic_index_in_dim(key_all, kv_index, 1, keepdims=False)
        value_head = lax.dynamic_index_in_dim(value_all, kv_index, 1, keepdims=False)
        offsets = lax.dynamic_index_in_dim(slash_offsets, head_index, 0, keepdims=False)
        unions = lax.dynamic_index_in_dim(union_blocks, kv_index, 0, keepdims=False)
        picks = lax.dynamic_index_in_dim(head_picks, head_index, 0, keepdims=False)
        counts = lax.dynamic_index_in_dim(owner_counts, head_index, 0, keepdims=False)
        blocks_flat = (owner_base + jnp.take_along_axis(unions, picks, axis=1)).reshape(-1).astype(jnp.int32)
        valid_flat = (jnp.arange(VPER, dtype=jnp.int32)[None, :] < counts[:, None]).reshape(-1)
        slot_count = blocks_flat.shape[0]
        key_blocks = key_head.reshape(count_of_blocks, BLOCK_TOKENS, HEAD_SIZE)
        value_blocks = value_head.reshape(count_of_blocks, BLOCK_TOKENS, HEAD_SIZE)
        vert_keys = key_blocks[blocks_flat].reshape(slot_count * BLOCK_TOKENS, HEAD_SIZE)
        vert_values = value_blocks[blocks_flat].reshape(slot_count * BLOCK_TOKENS, HEAD_SIZE)
        query_single_float = query_head.astype(jnp.float32)
        vert_scores = jnp.einsum("qd,kd->qk", query_single_float, vert_keys.astype(jnp.float32), precision=lax.Precision.HIGHEST) * scale_of_scores
        distance = query_block[:, None] - blocks_flat[None, :]
        on_slash = jnp.any(distance[:, :, None] == offsets[None, None, :], axis=2)
        block_mask = valid_flat[None, :] & jnp.logical_not(on_slash)
        key_place = (blocks_flat[:, None] * BLOCK_TOKENS + inner_offset[None, :]).reshape(-1)
        vert_mask = jnp.broadcast_to(block_mask[:, None, :, None], (count_of_blocks, BLOCK_TOKENS, slot_count, BLOCK_TOKENS)).reshape(SEQ, slot_count * BLOCK_TOKENS)
        vert_mask = vert_mask & (key_place[None, :] <= query_place[:, None])
        slash_index = query_block[:, None] - offsets[None, :]
        slash_valid = slash_index >= 0
        slash_block = jnp.maximum(slash_index, 0).astype(jnp.int32)
        diagonal_keys = key_blocks[slash_block]
        diagonal_values = value_blocks[slash_block]
        diagonal_scores = jnp.einsum("hax,hisx->hais", query_single_float.reshape(count_of_blocks, BLOCK_TOKENS, HEAD_SIZE), diagonal_keys.astype(jnp.float32), precision=lax.Precision.HIGHEST) * scale_of_scores
        slash_mask = slash_valid[:, None, :, None] & ((offsets[None, None, :, None] > 0) | (inner_offset[None, None, None, :] <= inner_offset[None, :, None, None]))
        slash_mask = jnp.broadcast_to(slash_mask, (count_of_blocks, BLOCK_TOKENS, NS, BLOCK_TOKENS)).reshape(SEQ, NS * BLOCK_TOKENS)
        return attend(vert_scores, vert_mask, diagonal_scores.reshape(SEQ, NS * BLOCK_TOKENS), slash_mask, vert_values, diagonal_values, count_of_blocks)

    per_head = lax.map(one_head, jnp.arange(HQ, dtype=jnp.int32))
    attended = per_head.transpose(1, 0, 2).reshape(SEQ, HQ * HEAD_SIZE)
    return jnp.dot(attended, out_weight, preferred_element_type=jnp.float32).astype(jnp.bfloat16)
```

```python
import functools

import jax
import jax.numpy as jnp
from jax import lax
from jax.experimental import pallas as pl
from jax.experimental.pallas import tpu as pltpu
from jax.sharding import PartitionSpec as P

HEAD_SIZE = 128
BLOCK = 64
NS = 4
HEADS = 4
OWNERS = 32
PER_DEV = 8
TOKENS = 512
NX, NZ, NY = 4, 8, 4
TILE = 256
NEAR = 6 * BLOCK
NEG = -1e30
SCALE = HEAD_SIZE**-0.5
MESH = pl.DeviceIdType.MESH


def kernel(
    slash, union, picks, counts, q_hbm, k_hbm, v_hbm, w_hbm, out_ref,
    q_ref, k_own, v_own, ke, ve, w_ref, pieces, kh, vh, scores, near_scores, near_probs, numer, att, acc,
    far_bias, local_sem, send_sem, recv_sem, ysend_sem, yrecv_sem,
):
    c = lax.axis_index("ctx")
    hd = lax.axis_index("head")
    x, z = c // NZ, lax.rem(c, NZ)
    y, core = hd // 2, lax.rem(hd, 2)

    def at_xz(dx, dz):
        return {"ctx": lax.rem(x + dx + NX, NX) * NZ + lax.rem(z + dz + NZ, NZ)}

    def at_y(dy):
        return {"head": lax.rem(y + dy + NY, NY) * 2 + core}

    sibling = {"head": y * 2 + 1 - core}
    after = {"ctx": lax.rem(c + 1, OWNERS)}
    before = {"ctx": lax.rem(c + OWNERS - 1, OWNERS)}

    k_in = pltpu.make_async_copy(k_hbm, ke.at[pl.ds(PER_DEV, PER_DEV)], local_sem.at[0])
    v_in = pltpu.make_async_copy(v_hbm, ve.at[pl.ds(PER_DEV, PER_DEV)], local_sem.at[1])
    q_in = pltpu.make_async_copy(q_hbm, q_ref, local_sem.at[2])
    w_in = pltpu.make_async_copy(w_hbm, w_ref, local_sem.at[3])
    k_pack = pltpu.make_async_copy(k_hbm, k_own, local_sem.at[4])
    v_pack = pltpu.make_async_copy(v_hbm, v_own, local_sem.at[5])
    for copy in (k_pack, v_pack, k_in, v_in, q_in, w_in):
        copy.start()

    barrier = pltpu.get_barrier_semaphore()
    peers = (
        at_xz(1, 0), at_xz(-1, 0), at_xz(0, 1), at_xz(0, -1), after, before,
        sibling, at_y(1), at_y(-1),
    )
    for peer in peers:
        pl.semaphore_signal(barrier, inc=1, device_id=peer, device_id_type=MESH)

    vh[:, HEAD_SIZE:] = jnp.ones((OWNERS * BLOCK, HEAD_SIZE), jnp.bfloat16)
    acc[...] = jnp.zeros_like(acc)

    k_pack.wait()
    v_pack.wait()
    own = (z * 8 + x * 2, 64 + x * 16 + z * 2)
    for u in range(2):
        pieces[own[u]] = k_own[union[0, u, c]]
        pieces[own[u] + 1] = v_own[union[0, u, c]]

    def remote(ref, at, size, sem, device):
        part = ref.at[pl.ds(at, size)]
        return pltpu.make_async_remote_copy(
            src_ref=part, dst_ref=part, send_sem=send_sem.at[sem], recv_sem=recv_sem.at[sem],
            device_id=device, device_id_type=MESH,
        )

    def xs(d):
        return lax.rem(x + d + 2 * NX, NX)

    def zs(d):
        return lax.rem(z + d + 2 * NZ, NZ)

    def a1(step, way, d):
        half = 0 if step == 1 else (0 if way > 0 else 1)
        size = 2 if step == 1 else 1
        sem = (step - 1) * 2 + (0 if way > 0 else 1)
        dev = at_xz(way, 0)
        return remote(pieces, z * 8 + xs(-way * d) * 2 + half, size, sem, dev)

    def b1(step, way, d):
        half = 0 if step < 4 else (0 if way > 0 else 1)
        size = 2 if step < 4 else 1
        sem = 4 + (step - 1) * 2 + (0 if way > 0 else 1)
        dev = at_xz(0, way)
        return remote(pieces, 64 + x * 16 + zs(-way * d) * 2 + half, size, sem, dev)

    def a2(step, way, d):
        half = 0 if step < 4 else (0 if way > 0 else 4)
        size = 8 if step < 4 else 4
        sem = 12 + (step - 1) * 2 + (0 if way > 0 else 1)
        dev = at_xz(0, way)
        return remote(pieces, zs(-way * d) * 8 + half, size, sem, dev)

    def b2(step, way, d):
        half = 0 if step == 1 else (0 if way > 0 else 8)
        size = 16 if step == 1 else 8
        sem = 20 + (step - 1) * 2 + (0 if way > 0 else 1)
        dev = at_xz(way, 0)
        return remote(pieces, 64 + xs(-way * d) * 16 + half, size, sem, dev)

    def previous(ref, sem):
        return pltpu.make_async_remote_copy(
            src_ref=ref.at[pl.ds(PER_DEV, PER_DEV)], dst_ref=ref.at[pl.ds(0, PER_DEV)],
            send_sem=send_sem.at[sem], recv_sem=recv_sem.at[sem],
            device_id=after, device_id_type=MESH,
        )

    pl.semaphore_wait(barrier, len(peers))

    def go(kind, step):
        for way in (1, -1):
            kind(step, way, step - 1).start()

    def come(kind, step):
        for way in (1, -1):
            kind(step, way, step).wait_recv()

    go(a1, 1)
    go(b1, 1)
    come(a1, 1)
    go(a1, 2)
    come(b1, 1)
    go(b1, 2)
    come(a1, 2)
    go(a2, 1)
    come(b1, 2)
    go(b1, 3)
    k_in.wait()
    v_in.wait()
    previous(ke, 24).start()
    previous(ve, 25).start()

    for j in range(HEADS):
        for o in range(OWNERS):
            seen = jnp.logical_and(counts[j, o] > 0, o <= c - 2)
            value = jnp.where(seen, 0.0, NEG).astype(jnp.float32)
            far_bias[j, :, o * BLOCK : (o + 1) * BLOCK] = jnp.full((8, BLOCK), value, jnp.float32)

    come(b1, 3)
    go(b1, 4)
    come(a2, 1)
    go(a2, 2)
    come(b1, 4)
    go(b2, 1)
    come(a2, 2)
    go(a2, 3)
    come(b2, 1)
    go(b2, 2)
    come(a2, 3)
    go(a2, 4)
    q_in.wait()
    previous(ke, 24).wait_recv()
    previous(ve, 25).wait_recv()
    come(b2, 2)
    come(a2, 4)

    lane = lax.broadcasted_iota(jnp.int32, (BLOCK, 2 * BLOCK), 1)
    row = lax.broadcasted_iota(jnp.int32, (BLOCK, 2 * BLOCK), 0)
    low = lane < BLOCK
    causal = jnp.where((lane % BLOCK) <= row, 0.0, NEG).astype(jnp.float32)
    c_before = jnp.maximum(c - 1, 0)
    ones = jnp.ones((NEAR, HEAD_SIZE), jnp.bfloat16)

    def picked(j, owner):
        first, second = union[0, 0, owner], union[0, 1, owner]
        return first + picks[j, 0, owner] * (second - first)

    def near_blocks(j, i):
        slashes = [i + PER_DEV - slash[j, s] for s in range(NS)]
        return slashes + [picked(j, c_before), PER_DEV + picked(j, c)]

    def attend(j):
        columns = pl.ds(pl.multiple_of(j * HEAD_SIZE, HEAD_SIZE), HEAD_SIZE)
        for o in range(OWNERS):
            first, second = (o % NZ) * 8 + (o // NZ) * 2, 64 + 2 * o
            at = first + picks[j, 0, o] * (second - first)
            kh[o * BLOCK : (o + 1) * BLOCK, :] = pieces[at]
            vh[o * BLOCK : (o + 1) * BLOCK, :HEAD_SIZE] = pieces[at + 1]

        def near(i, _):
            rows = pl.ds(pl.multiple_of(i * BLOCK, BLOCK), BLOCK)
            keys = jnp.concatenate([ke[b] for b in near_blocks(j, i)], axis=0)
            s = lax.dot_general(
                q_ref[rows, columns], keys, (((1,), (1,)), ((), ())), preferred_element_type=jnp.float32
            )
            hidden = []
            for t in range(NS):
                hidden.append(jnp.where(c * PER_DEV + i - slash[j, t] >= 0, 0.0, NEG).astype(jnp.float32))
            for owner, there, distance in (
                (c_before, c > 0, PER_DEV + i - picked(j, c_before)),
                (c, c >= 0, i - picked(j, c)),
            ):
                shown = jnp.logical_and(jnp.logical_and(counts[j, owner] > 0, there), distance > 0)
                for t in range(NS):
                    shown = jnp.logical_and(shown, distance != slash[j, t])
                hidden.append(jnp.where(shown, 0.0, NEG).astype(jnp.float32))
            diagonal = [jnp.where(slash[j, t] == 0, 1.0, 0.0).astype(jnp.float32) for t in range(NS)] + [None] * 2
            for g in range(3):
                bias = jnp.where(low, hidden[2 * g], hidden[2 * g + 1])
                if g < 2:
                    bias = bias + causal * jnp.where(low, diagonal[2 * g], diagonal[2 * g + 1])
                part = slice(g * 2 * BLOCK, (g + 1) * 2 * BLOCK)
                near_scores[rows, part] = s[:, part] + bias
            return 0

        lax.fori_loop(0, PER_DEV, near, 0)

        def far(tile, _):
            rows = pl.ds(pl.multiple_of(tile * TILE, TILE), TILE)
            queries = q_ref[rows, columns]
            peak = functools.reduce(
                jnp.maximum, [near_scores[rows, g * 128 : (g + 1) * 128] for g in range(3)]
            )
            for part in range(4):
                at = part * 512
                s = lax.dot_general(
                    queries, kh[at : at + 512, :], (((1,), (1,)), ((), ())), preferred_element_type=jnp.float32
                )
                s = s + far_bias[j, 0:1, at : at + 512]
                scores[:, at : at + 512] = s
                for g in range(4):
                    peak = jnp.maximum(peak, s[:, g * 128 : (g + 1) * 128])
            peak = jnp.max(peak, axis=1, keepdims=True) * SCALE
            total = jnp.zeros((TILE, 2 * HEAD_SIZE), jnp.float32)
            for part in range(4):
                at = part * 512
                p = jnp.exp(scores[:, at : at + 512] * SCALE - peak).astype(jnp.bfloat16)
                total = total + jnp.dot(p, vh[at : at + 512, :], preferred_element_type=jnp.float32)
            numer[rows, :] = total
            near_probs[rows, :] = jnp.exp(near_scores[rows, :] * SCALE - peak).astype(jnp.bfloat16)
            return 0

        lax.fori_loop(0, TOKENS // TILE, far, 0)

        def finish(i, _):
            rows = pl.ds(pl.multiple_of(i * BLOCK, BLOCK), BLOCK)
            values = jnp.concatenate([ve[b] for b in near_blocks(j, i)], axis=0)
            both = jnp.concatenate([values, ones], axis=1)
            full = numer[rows, :] + jnp.dot(near_probs[rows, :], both, preferred_element_type=jnp.float32)
            att[hd, j, rows, :] = (full[:, :HEAD_SIZE] / full[:, HEAD_SIZE:]).astype(jnp.bfloat16)
            return 0

        lax.fori_loop(0, PER_DEV, finish, 0)

    def source(dy, other=False):
        return lax.rem(y + dy + NY, NY) * 2 + (1 - core if other else core)

    def part(j, which, src, first, size, device):
        ref = att.at[src, j, pl.ds(first, size)]
        return pltpu.make_async_remote_copy(
            src_ref=ref, dst_ref=ref, send_sem=ysend_sem.at[j, which], recv_sem=yrecv_sem.at[j, which],
            device_id=device, device_id_type=MESH,
        )

    HALF = TOKENS // 2
    plan = (
        (source(0), source(0, True), 0, TOKENS, sibling),
        (source(0), source(-1), 0, TOKENS, at_y(1)),
        (source(0), source(1), 0, TOKENS, at_y(-1)),
        (source(-1), source(-2), 0, HALF, at_y(1)),
        (source(1), source(2), HALF, HALF, at_y(-1)),
        (source(-1), source(-1, True), 0, TOKENS, sibling),
        (source(1), source(1, True), 0, TOKENS, sibling),
        (source(2), source(2, True), 0, HALF, sibling),
        (source(2), source(2, True), HALF, HALF, sibling),
    )

    def y_go(j, *which):
        for n in which:
            src, _, first, size, device = plan[n]
            part(j, n, src, first, size, device).start()

    def y_come(j, *which):
        for n in which:
            _, src, first, size, device = plan[n]
            part(j, n, src, first, size, device).wait_recv()

    def send(j):
        y_go(j, 1, 2, 0)

    def relay(j):
        y_come(j, 1)
        y_go(j, 3, 5)
        y_come(j, 2)
        y_go(j, 4, 6)

    def relay_far(j):
        y_come(j, 3)
        y_go(j, 7)
        y_come(j, 4)
        y_go(j, 8)

    def project(j):
        y_come(j, 0, 5, 6, 7, 8)

        def tile(t, _):
            rows = pl.ds(pl.multiple_of(t * TILE, TILE), TILE)
            a = jnp.concatenate([att[s, j, rows, :] for s in range(8)], axis=1)
            w = jnp.concatenate([w_ref[s, j] for s in range(8)], axis=0)
            acc[rows, :] += jnp.dot(a, w, preferred_element_type=jnp.float32)
            return 0

        lax.fori_loop(0, TOKENS // TILE, tile, 0)

    w_in.wait()

    def stage(j, _):
        @pl.when(j < HEADS)
        def _():
            attend(j)
            send(j)

        @pl.when(jnp.logical_and(j >= 1, j <= HEADS))
        def _():
            relay(j - 1)

        @pl.when(jnp.logical_and(j >= 2, j <= HEADS + 1))
        def _():
            relay_far(j - 2)
            project(j - 2)

        return 0

    lax.fori_loop(0, HEADS + 2, stage, 0)
    out_ref[...] = acc[...].astype(jnp.bfloat16)

    for kind, steps in ((a1, 2), (b1, 4), (a2, 4), (b2, 2)):
        for step in range(1, steps + 1):
            for way in (1, -1):
                kind(step, way, step - 1).wait_send()
    previous(ke, 24).wait_send()
    previous(ve, 25).wait_send()

    def drain(j, _):
        for n in range(9):
            src, _, first, size, device = plan[n]
            part(j, n, src, first, size, device).wait_send()
        return 0

    lax.fori_loop(0, HEADS, drain, 0)


def shards(queries, key_rows, value_rows, slash_offsets, union_blocks, head_picks, owner_counts, out_weight):
    bf16, f32 = jnp.bfloat16, jnp.float32
    smem = pl.BlockSpec(memory_space=pltpu.SMEM)
    hbm = pl.BlockSpec(memory_space=pl.ANY)
    vmem = pltpu.VMEM
    return pl.pallas_call(
        kernel,
        out_shape=jax.ShapeDtypeStruct((TOKENS, TOKENS), bf16),
        in_specs=[smem] * 4 + [hbm] * 4,
        out_specs=pl.BlockSpec(memory_space=pltpu.VMEM),
        scratch_shapes=[
            vmem((TOKENS, HEADS * HEAD_SIZE), bf16),
            vmem((PER_DEV, BLOCK, HEAD_SIZE), bf16),
            vmem((PER_DEV, BLOCK, HEAD_SIZE), bf16),
            vmem((2 * PER_DEV, BLOCK, HEAD_SIZE), bf16),
            vmem((2 * PER_DEV, BLOCK, HEAD_SIZE), bf16),
            vmem((8, HEADS, HEAD_SIZE, TOKENS), bf16),
            vmem((128, BLOCK, HEAD_SIZE), bf16),
            vmem((OWNERS * BLOCK, HEAD_SIZE), bf16),
            vmem((OWNERS * BLOCK, 2 * HEAD_SIZE), bf16),
            vmem((TILE, OWNERS * BLOCK), f32),
            vmem((TOKENS, NEAR), f32),
            vmem((TOKENS, NEAR), bf16),
            vmem((TOKENS, 2 * HEAD_SIZE), f32),
            vmem((8, HEADS, TOKENS, HEAD_SIZE), bf16),
            vmem((TOKENS, TOKENS), f32),
            vmem((HEADS, 8, OWNERS * BLOCK), f32),
            pltpu.SemaphoreType.DMA((6,)),
            pltpu.SemaphoreType.DMA((26,)),
            pltpu.SemaphoreType.DMA((26,)),
            pltpu.SemaphoreType.DMA((HEADS, 9)),
            pltpu.SemaphoreType.DMA((HEADS, 9)),
        ],
        compiler_params=pltpu.CompilerParams(
            collective_id=0, has_side_effects=True, vmem_limit_bytes=60 * 1024 * 1024
        ),
    )(
        slash_offsets, union_blocks.transpose(0, 2, 1), head_picks.transpose(0, 2, 1), owner_counts,
        queries, key_rows.reshape(PER_DEV, BLOCK, HEAD_SIZE), value_rows.reshape(PER_DEV, BLOCK, HEAD_SIZE),
        out_weight.reshape(8, HEADS, HEAD_SIZE, TOKENS),
    )


def solution(mesh):
    in_specs = (
        P("ctx", "head"), P("ctx", "head"), P("ctx", "head"), P("head", None),
        P("head", None, None), P("head", None, None), P("head", None), P(None, "head"),
    )
    return jax.shard_map(
        shards, mesh=mesh, in_specs=in_specs, out_specs=P("ctx", "head"), check_vma=False
    )
```

```python
import functools

import jax
import jax.numpy as jnp
from jax import lax
from jax.experimental import pallas as pl
from jax.experimental.pallas import tpu as pltpu
from jax.sharding import PartitionSpec as P

HEAD_SIZE = 128
BLOCK = 64
NS = 4
HEADS = 4
OWNERS = 32
PER_DEV = 8
TOKENS = 512
NX, NZ, NY = 4, 8, 4
TILE = 256
TILES = TOKENS // TILE
UNITS = HEADS * TILES
NEAR = 6 * BLOCK
NEG = -1e30
SCALE = HEAD_SIZE**-0.5
MESH = pl.DeviceIdType.MESH

PLACE = [0, 1, 3, 5, 7, 6, 4, 2]
GROUPS = ((0, 1), (1, 2), (3, 2), (5, 3))


def kernel(
    slash, union, picks, counts, q_hbm, k_hbm, v_hbm, w_hbm, out_ref,
    q_ref, k_own, v_own, ke, ve, w_ref, pieces, kh, vh, scores, near_peak, near_sum, att, acc,
    far_bias, local_sem, send_sem, recv_sem, ysend_sem, yrecv_sem,
):
    c = lax.axis_index("ctx")
    hd = lax.axis_index("head")
    x, z = c // NZ, lax.rem(c, NZ)
    y, core = hd // 2, lax.rem(hd, 2)

    def at_xz(dx, dz):
        return {"ctx": lax.rem(x + dx + NX, NX) * NZ + lax.rem(z + dz + NZ, NZ)}

    def at_y(dy):
        return {"head": lax.rem(y + dy + NY, NY) * 2 + core}

    sibling = {"head": y * 2 + 1 - core}
    after = {"ctx": lax.rem(c + 1, OWNERS)}
    before = {"ctx": lax.rem(c + OWNERS - 1, OWNERS)}

    k_pack = pltpu.make_async_copy(k_hbm, k_own, local_sem.at[0])
    v_pack = pltpu.make_async_copy(v_hbm, v_own, local_sem.at[1])
    k_in = pltpu.make_async_copy(k_hbm, ke.at[pl.ds(PER_DEV, PER_DEV)], local_sem.at[2])
    v_in = pltpu.make_async_copy(v_hbm, ve.at[pl.ds(PER_DEV, PER_DEV)], local_sem.at[3])
    q_in = pltpu.make_async_copy(q_hbm, q_ref, local_sem.at[4])
    w_in = pltpu.make_async_copy(w_hbm, w_ref, local_sem.at[5])
    for copy in (k_pack, v_pack, k_in, v_in, q_in, w_in):
        copy.start()

    barrier = pltpu.get_barrier_semaphore()
    peers = [at_xz(0, dz) for dz in range(1, NZ)]
    peers += [at_xz(1, 0), at_xz(-1, 0), after, before, sibling, at_y(1), at_y(-1)]
    for peer in peers:
        pl.semaphore_signal(barrier, inc=1, device_id=peer, device_id_type=MESH)

    vh[:, HEAD_SIZE:] = jnp.ones((OWNERS * BLOCK, HEAD_SIZE), jnp.bfloat16)
    acc[...] = jnp.zeros_like(acc)

    def owner_of(dx, dz):
        return lax.rem(x + dx, NX) * NZ + lax.rem(z + dz, NZ)

    for dx in range(NX):
        for dz in range(NZ):
            o, at = owner_of(dx, dz), (dx * NZ + PLACE[dz]) * BLOCK
            for j in range(HEADS):
                seen = jnp.logical_and(counts[j, o] > 0, o <= c - 2)
                value = jnp.where(seen, 0.0, NEG).astype(jnp.float32)
                far_bias[j, :, at : at + BLOCK] = jnp.full((8, BLOCK), value, jnp.float32)

    k_pack.wait()
    v_pack.wait()
    for u in range(2):
        pieces[0, 2 * u] = k_own[union[0, u, c]]
        pieces[0, 2 * u + 1] = v_own[union[0, u, c]]

    def remote(src, dst, sem, device):
        return pltpu.make_async_remote_copy(
            src_ref=src, dst_ref=dst, send_sem=send_sem.at[sem], recv_sem=recv_sem.at[sem],
            device_id=device, device_id_type=MESH,
        )

    def along_z(dz):
        return remote(pieces.at[0], pieces.at[PLACE[NZ - dz]], dz - 1, at_xz(0, dz))

    def along_x(group, way):
        first, size = GROUPS[group]
        side = NX - 1 if way > 0 else 1
        return remote(
            pieces.at[pl.ds(first, size)], pieces.at[pl.ds(side * NZ + first, size)],
            7 + 2 * group + (way > 0), at_xz(way, 0),
        )

    def on_x(group, way):
        first, size = GROUPS[group]
        side, half = (NX - 1, 0) if way > 0 else (1, 2)
        return remote(
            pieces.at[pl.ds(side * NZ + first, size), pl.ds(half, 2)],
            pieces.at[pl.ds(2 * NZ + first, size), pl.ds(half, 2)],
            15 + 2 * group + (way > 0), at_xz(way, 0),
        )

    def previous(ref, sem):
        return remote(ref.at[pl.ds(PER_DEV, PER_DEV)], ref.at[pl.ds(0, PER_DEV)], sem, after)

    def z_come(*steps):
        for dz in steps:
            along_z(dz).wait_recv()

    def both_ways(kind, group):
        kind(group, 1).start()
        kind(group, -1).start()

    def x_come(kind, group):
        kind(group, 1).wait_recv()
        kind(group, -1).wait_recv()

    lane = lax.broadcasted_iota(jnp.int32, (BLOCK, 2 * BLOCK), 1)
    row = lax.broadcasted_iota(jnp.int32, (BLOCK, 2 * BLOCK), 0)
    low = lane < BLOCK
    causal = jnp.where((lane % BLOCK) <= row, 0.0, NEG).astype(jnp.float32)
    c_before = jnp.maximum(c - 1, 0)
    ones = jnp.ones((NEAR, HEAD_SIZE), jnp.bfloat16)

    def picked(j, owner):
        first, second = union[0, 0, owner], union[0, 1, owner]
        return first + picks[j, 0, owner] * (second - first)

    def near(i, _):
        rows = pl.ds(pl.multiple_of(i * BLOCK, BLOCK), BLOCK)
        for j in range(HEADS):
            blocks = [i + PER_DEV - slash[j, s] for s in range(NS)]
            blocks += [picked(j, c_before), PER_DEV + picked(j, c)]
            hidden = []
            for t in range(NS):
                hidden.append(jnp.where(c * PER_DEV + i - slash[j, t] >= 0, 0.0, NEG).astype(jnp.float32))
            for owner, there, distance in (
                (c_before, c > 0, PER_DEV + i - blocks[4]),
                (c, c >= 0, PER_DEV + i - blocks[5]),
            ):
                shown = jnp.logical_and(jnp.logical_and(counts[j, owner] > 0, there), distance > 0)
                for t in range(NS):
                    shown = jnp.logical_and(shown, distance != slash[j, t])
                hidden.append(jnp.where(shown, 0.0, NEG).astype(jnp.float32))
            diagonal = [jnp.where(slash[j, t] == 0, 1.0, 0.0).astype(jnp.float32) for t in range(NS)]
            keys = jnp.concatenate([ke[b] for b in blocks], axis=0)
            s = lax.dot_general(
                q_ref[rows, j * HEAD_SIZE : (j + 1) * HEAD_SIZE], keys, (((1,), (1,)), ((), ())),
                preferred_element_type=jnp.float32,
            )
            parts = []
            for g in range(3):
                bias = jnp.where(low, hidden[2 * g], hidden[2 * g + 1])
                if g < 2:
                    bias = bias + causal * jnp.where(low, diagonal[2 * g], diagonal[2 * g + 1])
                parts.append(s[:, g * 2 * BLOCK : (g + 1) * 2 * BLOCK] + bias)
            peak = jnp.max(functools.reduce(jnp.maximum, parts), axis=1, keepdims=True)
            near_peak[j, rows, :] = jnp.broadcast_to(peak, (BLOCK, HEAD_SIZE))
            peak = peak * SCALE
            p = jnp.concatenate([jnp.exp(part * SCALE - peak).astype(jnp.bfloat16) for part in parts], axis=1)
            values = jnp.concatenate([jnp.concatenate([ve[b] for b in blocks], axis=0), ones], axis=1)
            near_sum[j, rows, :] = jnp.dot(p, values, preferred_element_type=jnp.float32)
        return 0

    def near_rows(first, last):
        lax.fori_loop(first, last, near, 0)

    pl.semaphore_wait(barrier, len(peers))

    both_ways(along_x, 0)
    for dz in (1, 7, 2, 6):
        along_z(dz).start()
    k_in.wait()
    previous(ke, 23).start()
    for dz in (3, 5, 4):
        along_z(dz).start()
    v_in.wait()
    previous(ve, 24).start()
    q_in.wait()

    z_come(1, 7)
    both_ways(along_x, 1)
    x_come(along_x, 0)
    both_ways(on_x, 0)
    z_come(2, 6)
    both_ways(along_x, 2)
    z_come(3, 5, 4)
    both_ways(along_x, 3)
    x_come(along_x, 1)
    both_ways(on_x, 1)
    previous(ke, 23).wait_recv()
    previous(ve, 24).wait_recv()
    near_rows(0, 2)
    x_come(along_x, 2)
    both_ways(on_x, 2)
    near_rows(2, 4)
    x_come(along_x, 3)
    both_ways(on_x, 3)
    near_rows(4, 8)
    for group in range(4):
        x_come(on_x, group)
    w_in.wait()

    def attend(unit):
        j, tile = unit // TILES, lax.rem(unit, TILES)
        columns = pl.ds(pl.multiple_of(j * HEAD_SIZE, HEAD_SIZE), HEAD_SIZE)

        @pl.when(tile == 0)
        def _():
            for dx in range(NX):
                for dz in range(NZ):
                    slot = dx * NZ + PLACE[dz]
                    pick = picks[j, 0, owner_of(dx, dz)]
                    kh[slot * BLOCK : (slot + 1) * BLOCK, :] = pieces[slot, 2 * pick]
                    vh[slot * BLOCK : (slot + 1) * BLOCK, :HEAD_SIZE] = pieces[slot, 2 * pick + 1]

        rows = pl.ds(pl.multiple_of(tile * TILE, TILE), TILE)
        queries = q_ref[rows, columns]
        nearest = near_peak[j, rows, :]
        peak = nearest
        for part in range(4):
            at = part * 512
            s = lax.dot_general(
                queries, kh[at : at + 512, :], (((1,), (1,)), ((), ())), preferred_element_type=jnp.float32
            )
            s = s + far_bias[j, 0:1, at : at + 512]
            scores[:, at : at + 512] = s
            for g in range(4):
                peak = jnp.maximum(peak, s[:, g * 128 : (g + 1) * 128])
        peak = jnp.max(peak, axis=1, keepdims=True) * SCALE
        shrink = jnp.exp(nearest * SCALE - peak)
        total = near_sum[j, rows, :] * jnp.concatenate([shrink, shrink], axis=1)
        for part in range(4):
            at = part * 512
            p = jnp.exp(scores[:, at : at + 512] * SCALE - peak).astype(jnp.bfloat16)
            total = total + jnp.dot(p, vh[at : at + 512, :], preferred_element_type=jnp.float32)
        att[hd, j, rows, :] = (total[:, :HEAD_SIZE] / total[:, HEAD_SIZE:]).astype(jnp.bfloat16)

    def source(dy, other=False):
        return lax.rem(y + dy + NY, NY) * 2 + (1 - core if other else core)

    HALF = TILE // 2
    plan = (
        (source(0), source(0, True), 0, TILE, sibling),
        (source(0), source(-1), 0, TILE, at_y(1)),
        (source(0), source(1), 0, TILE, at_y(-1)),
        (source(-1), source(-2), 0, HALF, at_y(1)),
        (source(1), source(2), HALF, HALF, at_y(-1)),
        (source(-1), source(-1, True), 0, TILE, sibling),
        (source(1), source(1, True), 0, TILE, sibling),
        (source(2), source(2, True), 0, HALF, sibling),
        (source(2), source(2, True), HALF, HALF, sibling),
    )

    def exchange(unit, which, incoming):
        out, come, first, size, device = plan[which]
        j, tile = unit // TILES, lax.rem(unit, TILES)
        ref = att.at[come if incoming else out, j, pl.ds(pl.multiple_of(tile * TILE, TILE) + first, size)]
        return pltpu.make_async_remote_copy(
            src_ref=ref, dst_ref=ref, send_sem=ysend_sem.at[unit, which], recv_sem=yrecv_sem.at[unit, which],
            device_id=device, device_id_type=MESH,
        )

    def y_go(unit, *which):
        for n in which:
            exchange(unit, n, False).start()

    def y_come(unit, *which):
        for n in which:
            exchange(unit, n, True).wait_recv()

    def relay(unit):
        y_come(unit, 1)
        y_go(unit, 3, 5)
        y_come(unit, 2)
        y_go(unit, 4, 6)

    def relay_far(unit):
        y_come(unit, 3)
        y_go(unit, 7)
        y_come(unit, 4)
        y_go(unit, 8)

    def project(unit):
        y_come(unit, 0, 5, 6, 7, 8)
        j, tile = unit // TILES, lax.rem(unit, TILES)
        rows = pl.ds(pl.multiple_of(tile * TILE, TILE), TILE)
        a = jnp.concatenate([att[s, j, rows, :] for s in range(8)], axis=1)
        w = jnp.concatenate([w_ref[s, j] for s in range(8)], axis=0)
        acc[rows, :] += jnp.dot(a, w, preferred_element_type=jnp.float32)

    def stage(step, _):
        @pl.when(step < UNITS)
        def _():
            attend(step)
            y_go(step, 1, 2, 0)

        @pl.when(jnp.logical_and(step >= 2, step < UNITS + 2))
        def _():
            relay(step - 2)

        @pl.when(jnp.logical_and(step >= 4, step < UNITS + 4))
        def _():
            relay_far(step - 4)

        @pl.when(step >= 5)
        def _():
            project(step - 5)

        return 0

    lax.fori_loop(0, UNITS + 5, stage, 0)
    out_ref[...] = acc[...].astype(jnp.bfloat16)

    for dz in range(1, NZ):
        along_z(dz).wait_send()
    for group in range(4):
        for way in (1, -1):
            along_x(group, way).wait_send()
            on_x(group, way).wait_send()
    previous(ke, 23).wait_send()
    previous(ve, 24).wait_send()

    def drain(unit, _):
        for n in range(9):
            exchange(unit, n, False).wait_send()
        return 0

    lax.fori_loop(0, UNITS, drain, 0)


def shards(queries, key_rows, value_rows, slash_offsets, union_blocks, head_picks, owner_counts, out_weight):
    bf16, f32 = jnp.bfloat16, jnp.float32
    smem = pl.BlockSpec(memory_space=pltpu.SMEM)
    hbm = pl.BlockSpec(memory_space=pl.ANY)
    vmem, dma = pltpu.VMEM, pltpu.SemaphoreType.DMA
    blocks = (PER_DEV, BLOCK, HEAD_SIZE)
    return pl.pallas_call(
        kernel,
        out_shape=jax.ShapeDtypeStruct((TOKENS, TOKENS), bf16),
        in_specs=[smem] * 4 + [hbm] * 4,
        out_specs=pl.BlockSpec(memory_space=pltpu.VMEM),
        scratch_shapes=[
            vmem((TOKENS, HEADS * HEAD_SIZE), bf16),
            vmem(blocks, bf16),
            vmem(blocks, bf16),
            vmem((2 * PER_DEV, BLOCK, HEAD_SIZE), bf16),
            vmem((2 * PER_DEV, BLOCK, HEAD_SIZE), bf16),
            vmem((8, HEADS, HEAD_SIZE, TOKENS), bf16),
            vmem((OWNERS, 4, BLOCK, HEAD_SIZE), bf16),
            vmem((OWNERS * BLOCK, HEAD_SIZE), bf16),
            vmem((OWNERS * BLOCK, 2 * HEAD_SIZE), bf16),
            vmem((TILE, OWNERS * BLOCK), f32),
            vmem((HEADS, TOKENS, HEAD_SIZE), f32),
            vmem((HEADS, TOKENS, 2 * HEAD_SIZE), f32),
            vmem((8, HEADS, TOKENS, HEAD_SIZE), bf16),
            vmem((TOKENS, TOKENS), f32),
            vmem((HEADS, 8, OWNERS * BLOCK), f32),
            dma((6,)),
            dma((25,)),
            dma((25,)),
            dma((UNITS, 9)),
            dma((UNITS, 9)),
        ],
        compiler_params=pltpu.CompilerParams(
            collective_id=0, has_side_effects=True, vmem_limit_bytes=60 * 1024 * 1024
        ),
    )(
        slash_offsets, union_blocks.transpose(0, 2, 1), head_picks.transpose(0, 2, 1), owner_counts,
        queries, key_rows.reshape(blocks), value_rows.reshape(blocks),
        out_weight.reshape(8, HEADS, HEAD_SIZE, TOKENS),
    )


def solution(mesh):
    in_specs = (
        P("ctx", "head"), P("ctx", "head"), P("ctx", "head"), P("head", None),
        P("head", None, None), P("head", None, None), P("head", None), P(None, "head"),
    )
    return jax.shard_map(
        shards, mesh=mesh, in_specs=in_specs, out_specs=P("ctx", "head"), check_vma=False
    )
```

```python
import functools

import jax
import jax.numpy as jnp
from jax import lax
from jax.experimental import pallas as pl
from jax.experimental.pallas import tpu as pltpu
from jax.sharding import PartitionSpec as P

HEAD_SIZE = 128
BLOCK = 64
NS = 4
HEADS = 4
OWNERS = 32
PER_DEV = 8
TOKENS = 512
NX, NZ, NY = 4, 8, 4
TILE = 256
TILES = TOKENS // TILE
UNITS = HEADS * TILES
PART = 512
NEAR = 6 * BLOCK
NEG = -1e30
SCALE = HEAD_SIZE**-0.5
MESH = pl.DeviceIdType.MESH

PLACE = [0, 1, 3, 5, 7, 6, 4, 2]
GROUPS = ((0, 1), (1, 2), (3, 2), (5, 3))


def kernel(
    slash, union, picks, counts, q_hbm, k_hbm, v_hbm, w_hbm, out_ref,
    q_ref, k_own, v_own, ke, ve, w_ref, pieces, kt, vh, scores, near_peak, near_total, near_sum, att, acc,
    far_bias, local_sem, send_sem, recv_sem, ysend_sem, yrecv_sem,
):
    c = lax.axis_index("ctx")
    hd = lax.axis_index("head")
    x, z = c // NZ, lax.rem(c, NZ)
    y, core = hd // 2, lax.rem(hd, 2)

    def at_xz(dx, dz):
        return {"ctx": lax.rem(x + dx + NX, NX) * NZ + lax.rem(z + dz + NZ, NZ)}

    def at_y(dy):
        return {"head": lax.rem(y + dy + NY, NY) * 2 + core}

    sibling = {"head": y * 2 + 1 - core}
    after = {"ctx": lax.rem(c + 1, OWNERS)}
    before = {"ctx": lax.rem(c + OWNERS - 1, OWNERS)}

    k_pack = pltpu.make_async_copy(k_hbm, k_own, local_sem.at[0])
    v_pack = pltpu.make_async_copy(v_hbm, v_own, local_sem.at[1])
    k_in = pltpu.make_async_copy(k_hbm, ke.at[pl.ds(PER_DEV, PER_DEV)], local_sem.at[2])
    v_in = pltpu.make_async_copy(v_hbm, ve.at[pl.ds(PER_DEV, PER_DEV)], local_sem.at[3])
    q_in = pltpu.make_async_copy(q_hbm, q_ref, local_sem.at[4])
    w_in = pltpu.make_async_copy(w_hbm, w_ref, local_sem.at[5])
    for copy in (k_pack, v_pack, k_in, v_in, q_in, w_in):
        copy.start()

    barrier = pltpu.get_barrier_semaphore()
    peers = [at_xz(0, dz) for dz in (1, 2, 6, 7)]
    peers += [at_xz(1, 0), at_xz(-1, 0), after, before, sibling, at_y(1), at_y(-1)]
    for peer in peers:
        pl.semaphore_signal(barrier, inc=1, device_id=peer, device_id_type=MESH)

    acc[...] = jnp.zeros_like(acc)

    def owner_of(dx, dz):
        return lax.rem(x + dx, NX) * NZ + lax.rem(z + dz, NZ)

    for dx in range(NX):
        for dz in range(NZ):
            o, at = owner_of(dx, dz), (dx * NZ + PLACE[dz]) * BLOCK
            for j in range(HEADS):
                seen = jnp.logical_and(counts[j, o] > 0, o <= c - 2)
                value = jnp.where(seen, 0.0, NEG).astype(jnp.float32)
                far_bias[j, :, at : at + BLOCK] = jnp.full((8, BLOCK), value, jnp.float32)

    k_pack.wait()
    v_pack.wait()
    first, second, pick = union[0, 0, c], union[0, 1, c], picks[0, 0, c]
    for half, block in enumerate((first + pick * (second - first), second + pick * (first - second))):
        pieces[half, 0, 0] = k_own[block]
        pieces[half, 0, 1] = v_own[block]

    def remote(src, dst, sem, device):
        return pltpu.make_async_remote_copy(
            src_ref=src, dst_ref=dst, send_sem=send_sem.at[sem], recv_sem=recv_sem.at[sem],
            device_id=device, device_id_type=MESH,
        )

    def along_z(half, dz):
        return remote(pieces.at[half, 0], pieces.at[half, PLACE[NZ - dz]], 24 * half + dz - 1, at_xz(0, dz))

    def z_on(half, way):
        src, dst = (PLACE[6], PLACE[5]) if way > 0 else (PLACE[2], PLACE[3])
        return remote(
            pieces.at[half, src], pieces.at[half, dst], 24 * half + (2 if way > 0 else 4), at_xz(0, way)
        )

    def z_across(half, way):
        src, kind = (PLACE[6], 0) if way > 0 else (PLACE[2], 1)
        return remote(
            pieces.at[half, src, kind], pieces.at[half, PLACE[4], kind],
            24 * half + (3 if way > 0 else 7), at_xz(0, 2 * way),
        )

    def along_x(half, group, way):
        first, size = GROUPS[group]
        side = NX - 1 if way > 0 else 1
        return remote(
            pieces.at[half, pl.ds(first, size)], pieces.at[half, pl.ds(side * NZ + first, size)],
            24 * half + 8 + 2 * group + (way > 0), at_xz(way, 0),
        )

    def on_x(half, group, way):
        first, size = GROUPS[group]
        side, kind = (NX - 1, 0) if way > 0 else (1, 1)
        return remote(
            pieces.at[half, pl.ds(side * NZ + first, size), kind],
            pieces.at[half, pl.ds(2 * NZ + first, size), kind],
            24 * half + 16 + 2 * group + (way > 0), at_xz(way, 0),
        )

    def previous(ref, sem):
        return remote(ref.at[pl.ds(PER_DEV, PER_DEV)], ref.at[pl.ds(0, PER_DEV)], sem, after)

    def z_go(half, *steps):
        for dz in steps:
            along_z(half, dz).start()

    def z_come(half, *steps):
        for dz in steps:
            along_z(half, dz).wait_recv()

    def x_go(kind, half, group):
        kind(half, group, 1).start()
        kind(half, group, -1).start()

    def x_come(kind, half, group):
        kind(half, group, 1).wait_recv()
        kind(half, group, -1).wait_recv()

    def z_then_x(half, group, *steps):
        z_come(half, *steps)
        x_go(along_x, half, group)

    def z_far_go(half):
        z_come(half, 2, 6)
        for way in (1, -1):
            z_on(half, way).start()
            z_across(half, way).start()
        x_go(along_x, half, 2)

    def z_far_come(half):
        for way in (1, -1):
            z_on(half, way).wait_recv()
            z_across(half, way).wait_recv()
        x_go(along_x, half, 3)

    def further(half, group):
        x_come(along_x, half, group)
        x_go(on_x, half, group)

    lane = lax.broadcasted_iota(jnp.int32, (BLOCK, 2 * BLOCK), 1)
    row = lax.broadcasted_iota(jnp.int32, (BLOCK, 2 * BLOCK), 0)
    low = lane < BLOCK
    causal = jnp.where((lane % BLOCK) <= row, 0.0, NEG).astype(jnp.float32)
    c_before = jnp.maximum(c - 1, 0)

    def picked(j, owner):
        first, second = union[0, 0, owner], union[0, 1, owner]
        return first + picks[j, 0, owner] * (second - first)

    def near(i, _):
        rows = pl.ds(pl.multiple_of(i * BLOCK, BLOCK), BLOCK)
        for j in range(HEADS):
            blocks = [i + PER_DEV - slash[j, s] for s in range(NS)]
            blocks += [picked(j, c_before), PER_DEV + picked(j, c)]
            hidden = []
            for t in range(NS):
                hidden.append(jnp.where(c * PER_DEV + i - slash[j, t] >= 0, 0.0, NEG).astype(jnp.float32))
            for owner, there, distance in (
                (c_before, c > 0, PER_DEV + i - blocks[4]),
                (c, c >= 0, PER_DEV + i - blocks[5]),
            ):
                shown = jnp.logical_and(jnp.logical_and(counts[j, owner] > 0, there), distance > 0)
                for t in range(NS):
                    shown = jnp.logical_and(shown, distance != slash[j, t])
                hidden.append(jnp.where(shown, 0.0, NEG).astype(jnp.float32))
            diagonal = [jnp.where(slash[j, t] == 0, 1.0, 0.0).astype(jnp.float32) for t in range(NS)]
            keys = jnp.concatenate([ke[b] for b in blocks], axis=0)
            s = lax.dot_general(
                q_ref[rows, j * HEAD_SIZE : (j + 1) * HEAD_SIZE], keys, (((1,), (1,)), ((), ())),
                preferred_element_type=jnp.float32,
            )
            parts = []
            for g in range(3):
                bias = jnp.where(low, hidden[2 * g], hidden[2 * g + 1])
                if g < 2:
                    bias = bias + causal * jnp.where(low, diagonal[2 * g], diagonal[2 * g + 1])
                parts.append(s[:, g * 2 * BLOCK : (g + 1) * 2 * BLOCK] + bias)
            peak = jnp.max(functools.reduce(jnp.maximum, parts), axis=1, keepdims=True)
            near_peak[j, rows, :] = jnp.broadcast_to(peak, (BLOCK, HEAD_SIZE))
            peak = peak * SCALE
            weights = [jnp.exp(part * SCALE - peak) for part in parts]
            near_total[j, rows, :] = functools.reduce(jnp.add, weights)
            p = jnp.concatenate([w.astype(jnp.bfloat16) for w in weights], axis=1)
            values = jnp.concatenate([ve[b] for b in blocks], axis=0)
            near_sum[j, rows, :] = jnp.dot(p, values, preferred_element_type=jnp.float32)
        return 0

    def near_rows(first, last):
        lax.fori_loop(first, last, near, 0)

    pl.semaphore_wait(barrier, len(peers))

    x_go(along_x, 0, 0)
    z_go(0, 2, 6, 1, 7)
    k_in.wait()
    previous(ke, 48).start()
    v_in.wait()
    previous(ve, 49).start()
    z_far_go(0)
    z_then_x(0, 1, 1, 7)
    further(0, 0)
    z_far_come(0)
    x_go(along_x, 1, 0)
    z_go(1, 2, 6, 1, 7)
    further(0, 1)
    further(0, 2)
    q_in.wait()
    previous(ke, 48).wait_recv()
    previous(ve, 49).wait_recv()
    near_rows(0, 1)
    further(0, 3)
    near_rows(1, 2)
    z_far_go(1)
    near_rows(2, 3)
    z_then_x(1, 1, 1, 7)
    further(1, 0)
    near_rows(3, 4)
    z_far_come(1)
    near_rows(4, 5)
    further(1, 1)
    near_rows(5, 6)
    further(1, 2)
    near_rows(6, 7)
    further(1, 3)
    near_rows(7, 8)
    for group in range(4):
        x_come(on_x, 0, group)

    def rest():
        for group in range(4):
            x_come(on_x, 1, group)
        w_in.wait()

    def gather_blocks(which):
        for dx in range(NX):
            for place in range(0, NZ, 2):
                slot = dx * NZ + place
                halves = [which(owner_of(dx, PLACE.index(place + n))) for n in range(2)]
                keys = [pieces[halves[n], slot + n, 0] for n in range(2)]
                columns = slice(slot * BLOCK, (slot + 2) * BLOCK)
                kt[:, columns] = jnp.concatenate(keys, axis=0).T
                for n in range(2):
                    vh[(slot + n) * BLOCK : (slot + n + 1) * BLOCK, :] = pieces[halves[n], slot + n, 1]

    def attend(j):
        @pl.when(j == 0)
        def _():
            gather_blocks(lambda owner: 0)

        @pl.when(j > 0)
        def _():
            def which(owner):
                apart = picks[j, 0, owner] - picks[0, 0, owner]
                return apart * apart

            gather_blocks(which)

        columns = pl.ds(pl.multiple_of(j * HEAD_SIZE, HEAD_SIZE), HEAD_SIZE)

        for tile in range(TILES):
            rows = slice(tile * TILE, (tile + 1) * TILE)
            queries = q_ref[rows, columns]
            nearest = near_peak[j, rows, :]
            peak = nearest
            for at in range(0, OWNERS * BLOCK, PART):
                s = jnp.dot(queries, kt[:, at : at + PART], preferred_element_type=jnp.float32)
                s = s + far_bias[j, 0:1, at : at + PART]
                scores[rows, at : at + PART] = s
                for g in range(0, PART, 128):
                    peak = jnp.maximum(peak, s[:, g : g + 128])
            peak = jnp.max(peak, axis=1, keepdims=True) * SCALE
            shrink = jnp.exp(nearest * SCALE - peak)
            total = near_total[j, rows, :] * shrink
            numer = near_sum[j, rows, :] * shrink
            for at in range(0, OWNERS * BLOCK, PART):
                weights = jnp.exp(scores[rows, at : at + PART] * SCALE - peak)
                for g in range(0, PART, 128):
                    total = total + weights[:, g : g + 128]
                numer = numer + jnp.dot(
                    weights.astype(jnp.bfloat16), vh[at : at + PART, :], preferred_element_type=jnp.float32
                )
            att[hd, j, rows, :] = (numer / jnp.sum(total, axis=1, keepdims=True)).astype(jnp.bfloat16)

    def source(dy, other=False):
        return lax.rem(y + dy + NY, NY) * 2 + (1 - core if other else core)

    HALF = TILE // 2
    plan = (
        (source(0), source(0, True), 0, TILE, sibling),
        (source(0), source(-1), 0, TILE, at_y(1)),
        (source(0), source(1), 0, TILE, at_y(-1)),
        (source(-1), source(-2), 0, HALF, at_y(1)),
        (source(1), source(2), HALF, HALF, at_y(-1)),
        (source(-1), source(-1, True), 0, TILE, sibling),
        (source(1), source(1, True), 0, TILE, sibling),
        (source(2), source(2, True), 0, HALF, sibling),
        (source(2), source(2, True), HALF, HALF, sibling),
    )

    def exchange(unit, which, incoming):
        out, come, first, size, device = plan[which]
        j, tile = unit // TILES, lax.rem(unit, TILES)
        ref = att.at[come if incoming else out, j, pl.ds(pl.multiple_of(tile * TILE, TILE) + first, size)]
        return pltpu.make_async_remote_copy(
            src_ref=ref, dst_ref=ref, send_sem=ysend_sem.at[unit, which], recv_sem=yrecv_sem.at[unit, which],
            device_id=device, device_id_type=MESH,
        )

    def y_go(unit, *which):
        for n in which:
            exchange(unit, n, False).start()

    def y_come(unit, *which):
        for n in which:
            exchange(unit, n, True).wait_recv()

    def relay(unit):
        y_come(unit, 1)
        y_go(unit, 3, 5)
        y_come(unit, 2)
        y_go(unit, 4, 6)

    def relay_far(unit):
        y_come(unit, 3)
        y_go(unit, 7)
        y_come(unit, 4)
        y_go(unit, 8)

    def project(unit):
        y_come(unit, 0, 5, 6, 7, 8)
        j, tile = unit // TILES, lax.rem(unit, TILES)
        rows = pl.ds(pl.multiple_of(tile * TILE, TILE), TILE)
        a = jnp.concatenate([att[s, j, rows, :] for s in range(8)], axis=1)
        w = jnp.concatenate([w_ref[s, j] for s in range(8)], axis=0)
        acc[rows, :] += jnp.dot(a, w, preferred_element_type=jnp.float32)

    def of_head(do, head):
        for tile in range(TILES):
            do(TILES * head + tile)

    def stage(step, _):
        @pl.when(step == 1)
        def _():
            rest()

        @pl.when(step < HEADS)
        def _():
            attend(step)
            of_head(lambda unit: y_go(unit, 1, 2, 0), step)

        @pl.when(jnp.logical_or(step == 1, jnp.logical_and(step >= 3, step < HEADS + 2)))
        def _():
            of_head(relay, jnp.where(step == 1, 0, step - 2))

        @pl.when(jnp.logical_or(step == 2, jnp.logical_and(step >= 5, step < HEADS + 4)))
        def _():
            of_head(relay_far, jnp.where(step == 2, 0, step - 4))

        @pl.when(jnp.logical_or(step == 3, step >= 6))
        def _():
            of_head(project, jnp.where(step == 3, 0, step - 5))

        return 0

    lax.fori_loop(0, HEADS + 5, stage, 0)
    out_ref[...] = acc[...].astype(jnp.bfloat16)

    for half in range(2):
        for dz in (1, 2, 6, 7):
            along_z(half, dz).wait_send()
        for way in (1, -1):
            z_on(half, way).wait_send()
            z_across(half, way).wait_send()
        for group in range(4):
            for way in (1, -1):
                along_x(half, group, way).wait_send()
                on_x(half, group, way).wait_send()
    previous(ke, 48).wait_send()
    previous(ve, 49).wait_send()

    def drain(unit, _):
        for n in range(9):
            exchange(unit, n, False).wait_send()
        return 0

    lax.fori_loop(0, UNITS, drain, 0)


def shards(queries, key_rows, value_rows, slash_offsets, union_blocks, head_picks, owner_counts, out_weight):
    bf16, f32 = jnp.bfloat16, jnp.float32
    smem = pl.BlockSpec(memory_space=pltpu.SMEM)
    hbm = pl.BlockSpec(memory_space=pl.ANY)
    vmem, dma = pltpu.VMEM, pltpu.SemaphoreType.DMA
    blocks = (PER_DEV, BLOCK, HEAD_SIZE)
    return pl.pallas_call(
        kernel,
        out_shape=jax.ShapeDtypeStruct((TOKENS, TOKENS), bf16),
        in_specs=[smem] * 4 + [hbm] * 4,
        out_specs=pl.BlockSpec(memory_space=pltpu.VMEM),
        scratch_shapes=[
            vmem((TOKENS, HEADS * HEAD_SIZE), bf16),
            vmem(blocks, bf16),
            vmem(blocks, bf16),
            vmem((2 * PER_DEV, BLOCK, HEAD_SIZE), bf16),
            vmem((2 * PER_DEV, BLOCK, HEAD_SIZE), bf16),
            vmem((8, HEADS, HEAD_SIZE, TOKENS), bf16),
            vmem((2, OWNERS, 2, BLOCK, HEAD_SIZE), bf16),
            vmem((HEAD_SIZE, OWNERS * BLOCK), bf16),
            vmem((OWNERS * BLOCK, HEAD_SIZE), bf16),
            vmem((TOKENS, OWNERS * BLOCK), f32),
            vmem((HEADS, TOKENS, HEAD_SIZE), f32),
            vmem((HEADS, TOKENS, HEAD_SIZE), f32),
            vmem((HEADS, TOKENS, HEAD_SIZE), f32),
            vmem((8, HEADS, TOKENS, HEAD_SIZE), bf16),
            vmem((TOKENS, TOKENS), f32),
            vmem((HEADS, 8, OWNERS * BLOCK), f32),
            dma((6,)),
            dma((50,)),
            dma((50,)),
            dma((UNITS, 9)),
            dma((UNITS, 9)),
        ],
        compiler_params=pltpu.CompilerParams(
            collective_id=0, has_side_effects=True, vmem_limit_bytes=60 * 1024 * 1024
        ),
    )(
        slash_offsets, union_blocks.transpose(0, 2, 1), head_picks.transpose(0, 2, 1), owner_counts,
        queries, key_rows.reshape(blocks), value_rows.reshape(blocks),
        out_weight.reshape(8, HEADS, HEAD_SIZE, TOKENS),
    )


def solution(mesh):
    in_specs = (
        P("ctx", "head"), P("ctx", "head"), P("ctx", "head"), P("head", None),
        P("head", None, None), P("head", None, None), P("head", None), P(None, "head"),
    )
    return jax.shard_map(
        shards, mesh=mesh, in_specs=in_specs, out_specs=P("ctx", "head"), check_vma=False
    )
```

```python
import functools

import jax
import jax.numpy as jnp
from jax import lax
from jax.experimental import pallas as pl
from jax.experimental.pallas import tpu as pltpu
from jax.sharding import PartitionSpec as P

HEAD_SIZE = 128
BLOCK = 64
NS = 4
HEADS = 4
OWNERS = 32
PER_DEV = 8
TOKENS = 512
NX, NZ, NY = 4, 8, 4
TILE = 256
TILES = TOKENS // TILE
UNITS = HEADS * TILES
PART = 512
NEAR = 6 * BLOCK
NEG = -1e30
SCALE = HEAD_SIZE**-0.5
MESH = pl.DeviceIdType.MESH

PLACE = [0, 1, 3, 5, 7, 6, 4, 2]
GROUPS = ((0, 1), (1, 2), (3, 2), (5, 3))


def kernel(
    slash, union, picks, counts, q_hbm, k_hbm, v_hbm, w_hbm, out_ref,
    q_ref, k_own, v_own, ke, ve, w_ref, pieces, kt, vh, scores, near_peak, near_total, near_sum, att, acc,
    far_bias, local_sem, send_sem, recv_sem, ysend_sem, yrecv_sem,
):
    c = lax.axis_index("ctx")
    hd = lax.axis_index("head")
    x, z = c // NZ, lax.rem(c, NZ)
    y, core = hd // 2, lax.rem(hd, 2)

    def at_xz(dx, dz):
        return {"ctx": lax.rem(x + dx + NX, NX) * NZ + lax.rem(z + dz + NZ, NZ)}

    def at_y(dy):
        return {"head": lax.rem(y + dy + NY, NY) * 2 + core}

    sibling = {"head": y * 2 + 1 - core}
    after = {"ctx": lax.rem(c + 1, OWNERS)}
    before = {"ctx": lax.rem(c + OWNERS - 1, OWNERS)}

    k_pack = pltpu.make_async_copy(k_hbm, k_own, local_sem.at[0])
    v_pack = pltpu.make_async_copy(v_hbm, v_own, local_sem.at[1])
    k_in = pltpu.make_async_copy(k_hbm, ke.at[pl.ds(PER_DEV, PER_DEV)], local_sem.at[2])
    v_in = pltpu.make_async_copy(v_hbm, ve.at[pl.ds(PER_DEV, PER_DEV)], local_sem.at[3])
    q_in = pltpu.make_async_copy(q_hbm, q_ref, local_sem.at[4])
    w_in = pltpu.make_async_copy(w_hbm, w_ref, local_sem.at[5])
    for copy in (k_pack, v_pack, k_in, v_in, q_in, w_in):
        copy.start()

    barrier = pltpu.get_barrier_semaphore()
    peers = [at_xz(0, dz) for dz in (1, 2, 6, 7)]
    peers += [at_xz(1, 0), at_xz(-1, 0), after, before, sibling, at_y(1), at_y(-1)]
    for peer in peers:
        pl.semaphore_signal(barrier, inc=1, device_id=peer, device_id_type=MESH)

    acc[...] = jnp.zeros_like(acc)

    def owner_of(dx, dz):
        return lax.rem(x + dx, NX) * NZ + lax.rem(z + dz, NZ)

    for dx in range(NX):
        for dz in range(NZ):
            o, at = owner_of(dx, dz), (dx * NZ + PLACE[dz]) * BLOCK
            for j in range(HEADS):
                seen = jnp.logical_and(counts[j, o] > 0, o <= c - 2)
                value = jnp.where(seen, 0.0, NEG).astype(jnp.float32)
                far_bias[j, :, at : at + BLOCK] = jnp.full((8, BLOCK), value, jnp.float32)

    k_pack.wait()
    v_pack.wait()
    first, second, pick = union[0, 0, c], union[0, 1, c], picks[0, 0, c]
    for half, block in enumerate((first + pick * (second - first), second + pick * (first - second))):
        pieces[half, 0, 0] = k_own[block]
        pieces[half, 0, 1] = v_own[block]

    def remote(src, dst, sem, device):
        return pltpu.make_async_remote_copy(
            src_ref=src, dst_ref=dst, send_sem=send_sem.at[sem], recv_sem=recv_sem.at[sem],
            device_id=device, device_id_type=MESH,
        )

    def along_z(half, dz):
        return remote(pieces.at[half, 0], pieces.at[half, PLACE[NZ - dz]], 24 * half + dz - 1, at_xz(0, dz))

    def z_on(half, way):
        src, dst = (PLACE[6], PLACE[5]) if way > 0 else (PLACE[2], PLACE[3])
        return remote(
            pieces.at[half, src], pieces.at[half, dst], 24 * half + (2 if way > 0 else 4), at_xz(0, way)
        )

    def z_across(half, way):
        src, kind = (PLACE[6], 0) if way > 0 else (PLACE[2], 1)
        return remote(
            pieces.at[half, src, kind], pieces.at[half, PLACE[4], kind],
            24 * half + (3 if way > 0 else 7), at_xz(0, 2 * way),
        )

    def along_x(half, group, way):
        first, size = GROUPS[group]
        side = NX - 1 if way > 0 else 1
        return remote(
            pieces.at[half, pl.ds(first, size)], pieces.at[half, pl.ds(side * NZ + first, size)],
            24 * half + 8 + 2 * group + (way > 0), at_xz(way, 0),
        )

    def on_x(half, group, way):
        first, size = GROUPS[group]
        side, kind = (NX - 1, 0) if way > 0 else (1, 1)
        return remote(
            pieces.at[half, pl.ds(side * NZ + first, size), kind],
            pieces.at[half, pl.ds(2 * NZ + first, size), kind],
            24 * half + 16 + 2 * group + (way > 0), at_xz(way, 0),
        )

    def previous(ref, sem):
        return remote(ref.at[pl.ds(PER_DEV, PER_DEV)], ref.at[pl.ds(0, PER_DEV)], sem, after)

    def z_go(half, *steps):
        for dz in steps:
            along_z(half, dz).start()

    def z_come(half, *steps):
        for dz in steps:
            along_z(half, dz).wait_recv()

    def x_go(kind, half, group):
        kind(half, group, 1).start()
        kind(half, group, -1).start()

    def x_come(kind, half, group):
        kind(half, group, 1).wait_recv()
        kind(half, group, -1).wait_recv()

    def z_then_x(half, group, *steps):
        z_come(half, *steps)
        x_go(along_x, half, group)

    def z_far_go(half):
        z_come(half, 2, 6)
        for way in (1, -1):
            z_on(half, way).start()
            z_across(half, way).start()
        x_go(along_x, half, 2)

    def z_far_come(half):
        for way in (1, -1):
            z_on(half, way).wait_recv()
            z_across(half, way).wait_recv()
        x_go(along_x, half, 3)

    def further(half, group):
        x_come(along_x, half, group)
        x_go(on_x, half, group)

    lane = lax.broadcasted_iota(jnp.int32, (BLOCK, 2 * BLOCK), 1)
    row = lax.broadcasted_iota(jnp.int32, (BLOCK, 2 * BLOCK), 0)
    low = lane < BLOCK
    causal = jnp.where((lane % BLOCK) <= row, 0.0, NEG).astype(jnp.float32)
    c_before = jnp.maximum(c - 1, 0)

    def picked(j, owner):
        first, second = union[0, 0, owner], union[0, 1, owner]
        return first + picks[j, 0, owner] * (second - first)

    def near(i, _):
        rows = pl.ds(pl.multiple_of(i * BLOCK, BLOCK), BLOCK)
        for j in range(HEADS):
            blocks = [i + PER_DEV - slash[j, s] for s in range(NS)]
            blocks += [picked(j, c_before), PER_DEV + picked(j, c)]
            hidden = []
            for t in range(NS):
                hidden.append(jnp.where(c * PER_DEV + i - slash[j, t] >= 0, 0.0, NEG).astype(jnp.float32))
            for owner, there, distance in (
                (c_before, c > 0, PER_DEV + i - blocks[4]),
                (c, c >= 0, PER_DEV + i - blocks[5]),
            ):
                shown = jnp.logical_and(jnp.logical_and(counts[j, owner] > 0, there), distance > 0)
                for t in range(NS):
                    shown = jnp.logical_and(shown, distance != slash[j, t])
                hidden.append(jnp.where(shown, 0.0, NEG).astype(jnp.float32))
            diagonal = [jnp.where(slash[j, t] == 0, 1.0, 0.0).astype(jnp.float32) for t in range(NS)]
            keys = jnp.concatenate([ke[b] for b in blocks], axis=0)
            s = lax.dot_general(
                q_ref[rows, j * HEAD_SIZE : (j + 1) * HEAD_SIZE], keys, (((1,), (1,)), ((), ())),
                preferred_element_type=jnp.float32,
            )
            parts = []
            for g in range(3):
                bias = jnp.where(low, hidden[2 * g], hidden[2 * g + 1])
                if g < 2:
                    bias = bias + causal * jnp.where(low, diagonal[2 * g], diagonal[2 * g + 1])
                parts.append(s[:, g * 2 * BLOCK : (g + 1) * 2 * BLOCK] + bias)
            peak = jnp.max(functools.reduce(jnp.maximum, parts), axis=1, keepdims=True)
            near_peak[j, rows, :] = jnp.broadcast_to(peak, (BLOCK, HEAD_SIZE))
            peak = peak * SCALE
            weights = [jnp.exp(part * SCALE - peak) for part in parts]
            near_total[j, rows, :] = functools.reduce(jnp.add, weights)
            p = jnp.concatenate([w.astype(jnp.bfloat16) for w in weights], axis=1)
            values = jnp.concatenate([ve[b] for b in blocks], axis=0)
            near_sum[j, rows, :] = jnp.dot(p, values, preferred_element_type=jnp.float32)
        return 0

    def near_rows(first, last):
        lax.fori_loop(first, last, near, 0)

    pl.semaphore_wait(barrier, len(peers))

    x_go(along_x, 0, 0)
    z_go(0, 2, 6, 1, 7)
    k_in.wait()
    previous(ke, 48).start()
    v_in.wait()
    previous(ve, 49).start()
    z_far_go(0)
    z_then_x(0, 1, 1, 7)
    further(0, 0)
    z_far_come(0)
    x_go(along_x, 1, 0)
    z_go(1, 2, 6, 1, 7)
    further(0, 1)
    q_in.wait()
    previous(ke, 48).wait_recv()
    previous(ve, 49).wait_recv()
    near_rows(0, 1)
    further(0, 2)
    near_rows(1, 2)
    further(0, 3)
    near_rows(2, 3)
    z_far_go(1)
    near_rows(3, 4)
    z_then_x(1, 1, 1, 7)
    further(1, 0)
    near_rows(4, 5)
    z_far_come(1)
    near_rows(5, 6)
    further(1, 1)
    near_rows(6, 7)
    further(1, 2)
    near_rows(7, 8)
    further(1, 3)
    for group in range(4):
        x_come(on_x, 0, group)

    def rest():
        for group in range(4):
            x_come(on_x, 1, group)
        w_in.wait()

    def gather_blocks(which):
        for dx in range(NX):
            for place in range(0, NZ, 2):
                slot = dx * NZ + place
                halves = [which(owner_of(dx, PLACE.index(place + n))) for n in range(2)]
                keys = [pieces[halves[n], slot + n, 0] for n in range(2)]
                columns = slice(slot * BLOCK, (slot + 2) * BLOCK)
                kt[:, columns] = jnp.concatenate(keys, axis=0).T
                for n in range(2):
                    vh[(slot + n) * BLOCK : (slot + n + 1) * BLOCK, :] = pieces[halves[n], slot + n, 1]

    def attend(j):
        @pl.when(j == 0)
        def _():
            gather_blocks(lambda owner: 0)

        @pl.when(j > 0)
        def _():
            def which(owner):
                apart = picks[j, 0, owner] - picks[0, 0, owner]
                return apart * apart

            gather_blocks(which)

        columns = pl.ds(pl.multiple_of(j * HEAD_SIZE, HEAD_SIZE), HEAD_SIZE)

        for tile in range(TILES):
            rows = slice(tile * TILE, (tile + 1) * TILE)
            queries = q_ref[rows, columns]
            nearest = near_peak[j, rows, :]
            peak = nearest
            for at in range(0, OWNERS * BLOCK, PART):
                s = jnp.dot(queries, kt[:, at : at + PART], preferred_element_type=jnp.float32)
                s = s + far_bias[j, 0:1, at : at + PART]
                scores[rows, at : at + PART] = s
                for g in range(0, PART, 128):
                    peak = jnp.maximum(peak, s[:, g : g + 128])
            peak = jnp.max(peak, axis=1, keepdims=True) * SCALE
            shrink = jnp.exp(nearest * SCALE - peak)
            total = near_total[j, rows, :] * shrink
            numer = near_sum[j, rows, :] * shrink
            for at in range(0, OWNERS * BLOCK, PART):
                weights = jnp.exp(scores[rows, at : at + PART] * SCALE - peak)
                for g in range(0, PART, 128):
                    total = total + weights[:, g : g + 128]
                numer = numer + jnp.dot(
                    weights.astype(jnp.bfloat16), vh[at : at + PART, :], preferred_element_type=jnp.float32
                )
            att[hd, j, rows, :] = (numer / jnp.sum(total, axis=1, keepdims=True)).astype(jnp.bfloat16)
            y_go(TILES * j + tile, 1, 2, 0)

    def source(dy, other=False):
        return lax.rem(y + dy + NY, NY) * 2 + (1 - core if other else core)

    HALF = TILE // 2
    plan = (
        (source(0), source(0, True), 0, TILE, sibling),
        (source(0), source(-1), 0, TILE, at_y(1)),
        (source(0), source(1), 0, TILE, at_y(-1)),
        (source(-1), source(-2), 0, HALF, at_y(1)),
        (source(1), source(2), HALF, HALF, at_y(-1)),
        (source(-1), source(-1, True), 0, TILE, sibling),
        (source(1), source(1, True), 0, TILE, sibling),
        (source(2), source(2, True), 0, HALF, sibling),
        (source(2), source(2, True), HALF, HALF, sibling),
    )

    def exchange(unit, which, incoming):
        out, come, first, size, device = plan[which]
        j, tile = unit // TILES, lax.rem(unit, TILES)
        ref = att.at[come if incoming else out, j, pl.ds(pl.multiple_of(tile * TILE, TILE) + first, size)]
        return pltpu.make_async_remote_copy(
            src_ref=ref, dst_ref=ref, send_sem=ysend_sem.at[unit, which], recv_sem=yrecv_sem.at[unit, which],
            device_id=device, device_id_type=MESH,
        )

    def y_go(unit, *which):
        for n in which:
            exchange(unit, n, False).start()

    def y_come(unit, *which):
        for n in which:
            exchange(unit, n, True).wait_recv()

    def relay(unit):
        y_come(unit, 1)
        y_go(unit, 3, 5)
        y_come(unit, 2)
        y_go(unit, 4, 6)

    def relay_far(unit):
        y_come(unit, 3)
        y_go(unit, 7)
        y_come(unit, 4)
        y_go(unit, 8)

    def project(unit):
        y_come(unit, 0, 5, 6, 7, 8)
        j, tile = unit // TILES, lax.rem(unit, TILES)
        rows = pl.ds(pl.multiple_of(tile * TILE, TILE), TILE)
        a = jnp.concatenate([att[s, j, rows, :] for s in range(8)], axis=1)
        w = jnp.concatenate([w_ref[s, j] for s in range(8)], axis=0)
        acc[rows, :] += jnp.dot(a, w, preferred_element_type=jnp.float32)

    def of_head(do, head):
        for tile in range(TILES):
            do(TILES * head + tile)

    def stage(step, _):
        @pl.when(step == 1)
        def _():
            rest()

        @pl.when(step < HEADS)
        def _():
            attend(step)

        @pl.when(jnp.logical_or(step == 1, jnp.logical_and(step >= 3, step < HEADS + 2)))
        def _():
            of_head(relay, jnp.where(step == 1, 0, step - 2))

        @pl.when(jnp.logical_or(step == 2, jnp.logical_and(step >= 5, step < HEADS + 4)))
        def _():
            of_head(relay_far, jnp.where(step == 2, 0, step - 4))

        @pl.when(jnp.logical_or(step == 3, step >= 6))
        def _():
            of_head(project, jnp.where(step == 3, 0, step - 5))

        return 0

    lax.fori_loop(0, HEADS + 5, stage, 0)
    out_ref[...] = acc[...].astype(jnp.bfloat16)

    for half in range(2):
        for dz in (1, 2, 6, 7):
            along_z(half, dz).wait_send()
        for way in (1, -1):
            z_on(half, way).wait_send()
            z_across(half, way).wait_send()
        for group in range(4):
            for way in (1, -1):
                along_x(half, group, way).wait_send()
                on_x(half, group, way).wait_send()
    previous(ke, 48).wait_send()
    previous(ve, 49).wait_send()

    def drain(unit, _):
        for n in range(9):
            exchange(unit, n, False).wait_send()
        return 0

    lax.fori_loop(0, UNITS, drain, 0)


def shards(queries, key_rows, value_rows, slash_offsets, union_blocks, head_picks, owner_counts, out_weight):
    bf16, f32 = jnp.bfloat16, jnp.float32
    smem = pl.BlockSpec(memory_space=pltpu.SMEM)
    hbm = pl.BlockSpec(memory_space=pl.ANY)
    vmem, dma = pltpu.VMEM, pltpu.SemaphoreType.DMA
    blocks = (PER_DEV, BLOCK, HEAD_SIZE)
    return pl.pallas_call(
        kernel,
        out_shape=jax.ShapeDtypeStruct((TOKENS, TOKENS), bf16),
        in_specs=[smem] * 4 + [hbm] * 4,
        out_specs=pl.BlockSpec(memory_space=pltpu.VMEM),
        scratch_shapes=[
            vmem((TOKENS, HEADS * HEAD_SIZE), bf16),
            vmem(blocks, bf16),
            vmem(blocks, bf16),
            vmem((2 * PER_DEV, BLOCK, HEAD_SIZE), bf16),
            vmem((2 * PER_DEV, BLOCK, HEAD_SIZE), bf16),
            vmem((8, HEADS, HEAD_SIZE, TOKENS), bf16),
            vmem((2, OWNERS, 2, BLOCK, HEAD_SIZE), bf16),
            vmem((HEAD_SIZE, OWNERS * BLOCK), bf16),
            vmem((OWNERS * BLOCK, HEAD_SIZE), bf16),
            vmem((TOKENS, OWNERS * BLOCK), f32),
            vmem((HEADS, TOKENS, HEAD_SIZE), f32),
            vmem((HEADS, TOKENS, HEAD_SIZE), f32),
            vmem((HEADS, TOKENS, HEAD_SIZE), f32),
            vmem((8, HEADS, TOKENS, HEAD_SIZE), bf16),
            vmem((TOKENS, TOKENS), f32),
            vmem((HEADS, 8, OWNERS * BLOCK), f32),
            dma((6,)),
            dma((50,)),
            dma((50,)),
            dma((UNITS, 9)),
            dma((UNITS, 9)),
        ],
        compiler_params=pltpu.CompilerParams(
            collective_id=0, has_side_effects=True, vmem_limit_bytes=60 * 1024 * 1024
        ),
    )(
        slash_offsets, union_blocks.transpose(0, 2, 1), head_picks.transpose(0, 2, 1), owner_counts,
        queries, key_rows.reshape(blocks), value_rows.reshape(blocks),
        out_weight.reshape(8, HEADS, HEAD_SIZE, TOKENS),
    )


def solution(mesh):
    in_specs = (
        P("ctx", "head"), P("ctx", "head"), P("ctx", "head"), P("head", None),
        P("head", None, None), P("head", None, None), P("head", None), P(None, "head"),
    )
    return jax.shard_map(
        shards, mesh=mesh, in_specs=in_specs, out_specs=P("ctx", "head"), check_vma=False
    )
```
